128 devices in a mesh: row: 16 (over x, z_lo, core), col: 8 (over z_hi, y).
Axes of the slice: x: 4, y: 4, z: 4 (z_hi: 2, z_lo: 2; z = z_hi * 2 + z_lo), core: 2. Of those that a mesh axis runs over, the one named last changes fastest.
Arguments:
- features: bfloat16 [512, 8, 8192], P(None, 'col', 'row'), may hold values from 0 to 40
- block_values: bfloat16 [2, 16, 8, 320, 128, 128], P(None, 'row', 'col'), may hold values from -0.078125 to 0.078125
- block_rows: int32 [2, 16, 8, 320], P(None, 'row', 'col'), may hold values from 0 to 63, as said below
- block_cols: int32 [2, 16, 8, 320], P(None, 'row', 'col'), may hold values from 0 to 31
- block_counts: int32 [2, 16, 8], P(None, 'row', 'col'), may hold values from 80 to 320, as said below
- bias: float32 [2, 8, 8192], P(None, 'col', 'row'), may hold values from -1 to 0
Outputs:
- activations: bfloat16 [512, 8, 8192], P(None, 'col', 'row')
The draws below stay inside these ranges and needn't reach their ends.
Inputs may be any that keep to these rules, and one draw needn't show every extreme that they name: `block_rows`: each device's live slots in a layer name distinct block positions. `block_counts`: in every layer some device has all 320 slots live.
All inputs are finite; a program needn't handle non-finite values.
Results may differ from the reference program's by a relative error of at most 0.0036.
Values may be sent and summed in bfloat16 or wider, within the bound.
No kernel may reach another device: no remote copies, remote signals or barrier semaphores. Data moves between devices by JAX's collectives and lax.ppermute only.
A program may use at most 192 MiB of HBM per device.

```python
import jax
import jax.numpy as jnp
from jax import lax

N = 65536
BLK = 128
BATCH = 512
K = 320
LAYERS = 2
RB = 64
CB = 32
N_ROW = 16
N_COL = 8


def slot_positions(key):
    device_keys = jax.random.split(key, LAYERS * N_ROW * N_COL)
    position = jax.vmap(lambda one_key: jax.random.permutation(one_key, RB * CB)[:K])(device_keys)
    return position.astype(jnp.int32).reshape(LAYERS, N_ROW, N_COL, K)


def draw_block_rows(key, part):
    position = slot_positions(key)
    return (position // CB).astype(jnp.int32)


def draw_block_cols(key, part):
    position = slot_positions(key)
    return (position % CB).astype(jnp.int32)


def draw_block_counts(key, part):
    key = jax.random.fold_in(key, 7)
    first_key, second_key = jax.random.split(key)
    uniform_ints = jax.random.randint(first_key, (LAYERS, N_ROW * N_COL), 0, 1025)
    counts_drawn = K // 4 + (K - K // 4) * uniform_ints * uniform_ints // (1024 * 1024)
    chosen = jax.random.randint(second_key, (LAYERS, 1), 0, N_ROW * N_COL)
    spots = jnp.arange(N_ROW * N_COL, dtype=jnp.int32)[None, :]
    counts_drawn = jnp.where(spots == chosen, K, counts_drawn)
    lowest_spot = (chosen + 1) % (N_ROW * N_COL)
    counts_drawn = jnp.where(spots == lowest_spot, K // 4, counts_drawn)
    return counts_drawn.astype(jnp.int32).reshape(LAYERS, N_ROW, N_COL)


def block_levels(stream_key, shape, pieces, least, largest):
    factor_of = 1.0
    for dim, shards_of in pieces:
        steps = jax.random.uniform(jax.random.fold_in(jax.random.fold_in(stream_key, 6), dim), (shards_of,), jnp.float32, least / len(pieces), largest / len(pieces))
        factor_of = factor_of * jnp.repeat(jnp.exp(steps), shape[dim] // shards_of).reshape((-1,) + (1,) * (len(shape) - 1 - dim))
    return factor_of


def noise(key, dims, spread, limit, cuts=(), kind=jnp.bfloat16):
    loudness = block_levels(key, dims, cuts, -0.22, 0.18) if cuts else 1.0
    drawn = jax.random.normal(key, dims, jnp.float32) * spread * loudness
    return jnp.minimum(jnp.maximum(drawn, -limit), limit).astype(kind)


def setup_inputs(seed: int = 0) -> dict:
    key_of = jax.random.split(jax.random.key(seed), 7)
    features = jnp.clip(40.0 * jax.random.uniform(key_of[0], (BATCH, N_COL, N // N_COL), jnp.float32) ** block_levels(key_of[0], (BATCH, N_COL, N // N_COL), ((1, 8), (2, 16)), -0.2, 0.2), 0.0, 40.0).astype(jnp.bfloat16)
    block_values = noise(key_of[1], (LAYERS, N_ROW, N_COL, K, BLK, BLK), (BLK * K * N_COL // (2 * CB)) ** -0.5, 0.078125, ((1, 16), (2, 8)))
    block_rows = draw_block_rows(jax.random.fold_in(key_of[6], 71), 0)
    block_cols = draw_block_cols(jax.random.fold_in(key_of[6], 71), 0)
    block_counts = draw_block_counts(jax.random.fold_in(key_of[6], 71), 0)
    bias = jnp.clip(-1.0 + 1.0 * jax.random.uniform(key_of[5], (LAYERS, N_COL, N // N_COL), jnp.float32) ** block_levels(key_of[5], (LAYERS, N_COL, N // N_COL), ((1, 8), (2, 16)), -0.2, 0.2), -1.0, 0.0)
    return dict(features=features, block_values=block_values, block_rows=block_rows, block_cols=block_cols, block_counts=block_counts, bias=bias)


def layer_sums(current, values, slot_rows, slot_cols, live_counts):
    def one_row(row_index):
        def one_col(running, col_index):
            panel_now = lax.dynamic_index_in_dim(current, col_index, 1, keepdims=False)

            def one_slot(inner, slot_index):
                block_row = slot_rows[row_index, col_index, slot_index]
                block_col = slot_cols[row_index, col_index, slot_index]
                left_rows = lax.dynamic_slice_in_dim(panel_now, block_row * BLK, BLK, 1)
                product = jnp.dot(left_rows, values[row_index, col_index, slot_index], preferred_element_type=jnp.float32)
                product = jnp.where(slot_index < live_counts[row_index, col_index], product, jnp.zeros_like(product))
                present = lax.dynamic_slice_in_dim(inner, block_col * BLK, BLK, 1)
                return lax.dynamic_update_slice_in_dim(inner, present + product, block_col * BLK, 1), None

            running, _ = lax.scan(one_slot, running, jnp.arange(K, dtype=jnp.int32))
            return running, None

        start_sum = jnp.zeros((BATCH, N // N_ROW), jnp.float32)
        summed, _ = lax.scan(one_col, start_sum, jnp.arange(N_COL, dtype=jnp.int32))
        return summed

    return lax.map(one_row, jnp.arange(N_ROW, dtype=jnp.int32))


def reference(features, block_values, block_rows, block_cols, block_counts, bias):
    segment = N // (N_ROW * N_COL)
    current = features
    for layer_index in range(LAYERS):
        sums = layer_sums(current, block_values[layer_index], block_rows[layer_index], block_cols[layer_index], block_counts[layer_index])
        sums = sums.reshape(N_ROW, BATCH, N_COL, segment).transpose(1, 2, 0, 3).reshape(BATCH, N_COL, N // N_COL)
        current = jnp.clip(sums + bias[layer_index], 0.0, 32.0).astype(jnp.bfloat16)
    return current
```

```python
import functools

import jax
import jax.numpy as jnp
from jax import lax
from jax.experimental import pallas as pl
from jax.experimental.pallas import tpu as pltpu
from jax.sharding import PartitionSpec as P

BLK = 128
CB = 32
N_ROW = 16
N_COL = 8
N_X = 4
N_Y = 4
SUB = CB // N_COL
GROUP = 32
UNROLL = 16
HEIGHTS = (256, 256)
GATHER = 'sc'
GATE = False
ORDER = True
STEPS = 16.0
TOP = 32000.0
VMEM = pl.BlockSpec(memory_space=pltpu.VMEM)
SMEM = pl.BlockSpec(memory_space=pltpu.SMEM)
ANY = pl.BlockSpec(memory_space=pl.ANY)
HBM = pl.BlockSpec(memory_space=pltpu.HBM)

TO_Z_LO = [(r, r ^ 2) for r in range(N_ROW)]
TO_CORE = [(r, r ^ 1) for r in range(N_ROW)]
TO_Z_HI = [(c, c ^ 4) for c in range(N_COL)]


def from_x(d):
    return [(r, (r - 4 * d) % N_ROW) for r in range(N_ROW)]


def to_y(d):
    return [(c, (c & 4) + ((c + d) & 3)) for c in range(N_COL)]


def product_kernel(n_parts, layer, place, col, info, *refs):
    parts, (values, *refs) = refs[:n_parts], refs[n_parts:]
    *outs, panel, held, acc, part_sems, sems = refs[-N_COL - 5 :]
    height = panel.shape[1]
    count = info[0]
    groups = (count + GROUP - 1) // GROUP

    def weights(group):
        spot = pl.ds(group * GROUP, GROUP)
        return pltpu.make_async_copy(values.at[layer, 0, 0, spot], held.at[spot], sems.at[group])

    copies = [
        pltpu.make_async_copy(
            part, panel if len(part.shape) == 3 else panel.at[i], part_sems.at[i]
        )
        for i, part in enumerate(parts)
    ]
    for copy in copies:
        copy.start()

    def begin(group, _):
        weights(group).start()
        return 0

    lax.fori_loop(0, groups, begin, 0)
    acc[...] = jnp.zeros_like(acc)
    for copy in copies:
        copy.wait()

    def one_group(group, _):
        weights(group).wait()

        def one_step(step, _):
            for u in range(UNROLL):
                slot = group * GROUP + step * UNROLL + u
                where_at = place[slot]
                lanes = pl.ds(pl.multiple_of((where_at & (SUB - 1)) * BLK, BLK), BLK)
                left = panel[where_at >> 2, :, lanes]
                acc[col[slot]] += jnp.dot(left, held[slot], preferred_element_type=jnp.float32)
            return 0

        steps = (jnp.minimum(count - group * GROUP, GROUP) + UNROLL - 1) // UNROLL
        return lax.fori_loop(0, steps, one_step, 0)

    lax.fori_loop(0, groups, one_group, 0)

    for e in range(2):
        for d in range(N_Y):
            share = (info[1] ^ e) * N_Y + ((info[2] + d) & 3)
            encode(lambda t, share=share: acc[share * SUB + t], outs[e * N_Y + d], height)


def encode(sums_of, out, height):
    codes = []
    for t in range(SUB):
        sums = sums_of(t)
        most = jnp.max(jnp.abs(sums), axis=0, keepdims=True)
        code = jnp.ceil(jnp.log2(jnp.maximum(most, 1e-30)) * STEPS)
        codes.append(code)
        inverse = TOP * jnp.exp2(code * (-1.0 / STEPS))
        whole = jnp.round(sums * inverse).astype(jnp.int32)
        out[pl.ds(t * height, height), :] = whole.astype(jnp.int16)
    codes = jnp.concatenate(codes + [jnp.zeros((16 - SUB, BLK), jnp.float32)], axis=0)
    out[pl.ds(SUB * height, 16), :] = codes.astype(jnp.int32).astype(jnp.int16)


def product_vmem(height, slots):
    panel = N_ROW * height * SUB * BLK * 2
    totals = (CB + 1) * height * BLK * 4
    outs = N_COL * (SUB * height + 16) * BLK * 2
    return panel + totals + outs + slots * BLK * BLK * 2 + (3 << 20)


def product(layer, place, col, info, parts, values, height, after):
    slots = values.shape[3]
    piece = jax.ShapeDtypeStruct((SUB * height + 16, BLK), jnp.int16)
    return pl.pallas_call(
        functools.partial(product_kernel, len(parts), layer),
        out_shape=(piece,) * N_COL,
        in_specs=[SMEM] * 3 + [HBM] * (len(parts) + 1) + [ANY] * len(after),
        out_specs=(VMEM,) * N_COL,
        scratch_shapes=[
            pltpu.VMEM((N_ROW, height, SUB * BLK), jnp.bfloat16),
            pltpu.VMEM((slots, BLK, BLK), jnp.bfloat16),
            pltpu.VMEM((CB + 1, height, BLK), jnp.float32),
            pltpu.SemaphoreType.DMA((len(parts),)),
            pltpu.SemaphoreType.DMA((slots // GROUP,)),
        ],
        compiler_params=pltpu.CompilerParams(vmem_limit_bytes=58 * 1024 * 1024),
        cost_estimate=pl.CostEstimate(
            flops=4 * 2 * height * BLK * BLK * slots,
            bytes_accessed=slots * BLK * BLK * 2,
            transcendentals=0,
        ),
        name="product",
    )(place, col, info, *parts, values, *after)


def rows_at_once(height):
    return next(r for r in (64, 48, 32, 16) if height % r == 0)


def scales_of(piece, height):
    codes = piece[pl.ds(SUB * height, 16), :].astype(jnp.int32).astype(jnp.float32)
    return jnp.exp2(codes * (1.0 / STEPS)) * (1.0 / TOP)


def add_pieces(pieces, scales, t, spot):
    total = None
    for piece, scale in zip(pieces, scales):
        term = piece[spot, :].astype(jnp.int32).astype(jnp.float32) * scale[t : t + 1, :]
        total = term if total is None else total + term
    return total


def middle_kernel(a, b, c, d, out, totals):
    height = totals.shape[0]
    rows = rows_at_once(height)
    pieces = (a, b, c, d)
    scales = [scales_of(piece, height) for piece in pieces]
    codes = []
    for t in range(SUB):

        def add(i, most, t=t):
            first = pl.multiple_of(i * rows, rows)
            total = add_pieces(pieces, scales, t, pl.ds(t * height + first, rows))
            totals[pl.ds(first, rows), :] = total
            return jnp.maximum(most, jnp.max(jnp.abs(total).reshape(rows // 8, 8, BLK), axis=0))

        most = lax.fori_loop(0, height // rows, add, jnp.zeros((8, BLK), jnp.float32))
        most = jnp.max(most, axis=0, keepdims=True)
        code = jnp.ceil(jnp.log2(jnp.maximum(most, 1e-30)) * STEPS)
        codes.append(code)
        inverse = TOP * jnp.exp2(code * (-1.0 / STEPS))

        def store(i, _, t=t, inverse=inverse):
            first = pl.multiple_of(i * rows, rows)
            whole = jnp.round(totals[pl.ds(first, rows), :] * inverse).astype(jnp.int32)
            out[pl.ds(t * height + first, rows), :] = whole.astype(jnp.int16)
            return 0

        lax.fori_loop(0, height // rows, store, 0)
    codes = jnp.concatenate(codes + [jnp.zeros((16 - SUB, BLK), jnp.float32)], axis=0)
    out[pl.ds(SUB * height, 16), :] = codes.astype(jnp.int32).astype(jnp.int16)


def middle(pieces):
    height = (pieces[0].shape[0] - 16) // SUB
    return pl.pallas_call(
        middle_kernel,
        out_shape=jax.ShapeDtypeStruct(pieces[0].shape, jnp.int16),
        in_specs=[VMEM] * 4,
        out_specs=VMEM,
        scratch_shapes=[pltpu.VMEM((height, BLK), jnp.float32)],
        cost_estimate=pl.CostEstimate(
            flops=16 * pieces[0].size, bytes_accessed=8 * pieces[0].size, transcendentals=0
        ),
        name="middle",
    )(*pieces)


def add_and_clip(pieces, bias, out, height):
    rows = rows_at_once(height)
    scales = [scales_of(piece, height) for piece in pieces]
    for t in range(SUB):
        lanes = slice(t * BLK, (t + 1) * BLK)

        def part(i, _, t=t, lanes=lanes):
            first = pl.multiple_of(i * rows, rows)
            total = add_pieces(pieces, scales, t, pl.ds(t * height + first, rows)) + bias[:, lanes]
            kept = jnp.minimum(jnp.maximum(total, 0.0), 32.0)
            out[pl.ds(first, rows), lanes] = kept.astype(jnp.bfloat16)
            return 0

        lax.fori_loop(0, height // rows, part, 0)


def combine_kernel(a, b, c, d, other, bias, out, kept, sem):
    add_and_clip((a, b, c, d, other), bias, kept, kept.shape[0])
    copy = pltpu.make_async_copy(kept, out, sem)
    copy.start()
    copy.wait()


def finish_kernel(first, a, b, c, d, other, bias, *refs):
    out, kept, sem = refs[-3:]
    pieces = (a, b, c, d, other)
    add_and_clip(pieces, bias, kept, kept.shape[0])
    copy = pltpu.make_async_copy(kept, out.at[pl.ds(first, kept.shape[0])], sem)
    copy.start()
    copy.wait()


def combine(pieces, other, bias):
    height = (other.shape[0] - 16) // SUB
    return pl.pallas_call(
        combine_kernel,
        out_shape=jax.ShapeDtypeStruct((height, SUB * BLK), jnp.bfloat16),
        in_specs=[VMEM] * 6,
        out_specs=HBM,
        scratch_shapes=[
            pltpu.VMEM((height, SUB * BLK), jnp.bfloat16),
            pltpu.SemaphoreType.DMA,
        ],
        cost_estimate=pl.CostEstimate(
            flops=16 * other.size, bytes_accessed=10 * other.size, transcendentals=0
        ),
        name="combine",
    )(*pieces, other, bias)


def finish(pieces, other, bias, first, batch, earlier):
    height = (other.shape[0] - 16) // SUB
    more = [] if earlier is None else [earlier]
    return pl.pallas_call(
        functools.partial(finish_kernel, first),
        out_shape=jax.ShapeDtypeStruct((batch, SUB * BLK), jnp.bfloat16),
        in_specs=[VMEM] * 6 + [ANY] * len(more),
        out_specs=ANY,
        scratch_shapes=[
            pltpu.VMEM((height, SUB * BLK), jnp.bfloat16),
            pltpu.SemaphoreType.DMA,
        ],
        input_output_aliases={6: 0} if more else {},
        cost_estimate=pl.CostEstimate(
            flops=16 * other.size, bytes_accessed=10 * other.size, transcendentals=0
        ),
        name="finish",
    )(*pieces, other, bias, *more)


def take_kernel(first, whole, *refs):
    out, held, sem = refs[-3:]
    rows = pl.ds(first, out.shape[0])
    for copy in (
        pltpu.make_async_copy(whole.at[rows], held, sem),
        pltpu.make_async_copy(held, out, sem),
    ):
        copy.start()
        copy.wait()


def take(whole, first, height, after):
    return pl.pallas_call(
        functools.partial(take_kernel, first),
        out_shape=jax.ShapeDtypeStruct((height,) + whole.shape[1:], whole.dtype),
        in_specs=[ANY] * (1 + len(after)),
        out_specs=HBM,
        scratch_shapes=[
            pltpu.VMEM((height,) + whole.shape[1:], whole.dtype),
            pltpu.SemaphoreType.DMA,
        ],
        name="take",
    )(whole, *after)


def gather(current, gate):
    if GATHER == "sc":
        return [lax.all_gather(current, "row", axis=0, tiled=False)]
    near = [current] + [lax.ppermute(current, "row", from_x(d)) for d in range(1, N_X)]
    other = lax.ppermute(current, "row", TO_Z_LO)
    if gate:
        other = take(other, 0, other.shape[0], gate)
    far = [other] + [lax.ppermute(other, "row", from_x(d)) for d in range(1, N_X)]
    mine = [part for both in zip(near, far) for part in both]
    return mine + [lax.ppermute(part, "row", TO_CORE) for part in mine]


def on_device(features, block_values, block_rows, block_cols, block_counts, bias):
    layers, slots = block_values.shape[0], block_values.shape[3]
    batch = features.shape[0]
    here, there = lax.axis_index("row"), lax.axis_index("col")
    counts = block_counts[:, 0, 0]
    live = jnp.arange(slots, dtype=jnp.int32)[None, :] < counts[:, None]
    col = jnp.where(live, block_cols[:, 0, 0], CB)
    absolute = block_rows[:, 0, 0]
    shard, sub = absolute >> 2, absolute & 3
    apart_x = ((shard >> 2) - (here >> 2)) & 3
    apart_z = ((shard >> 1) ^ (here >> 1)) & 1
    apart_core = (shard ^ here) & 1
    place = (((apart_core * 4 + apart_x) * 2 + apart_z) << 2) + sub
    firsts = [sum(HEIGHTS[:c]) for c in range(len(HEIGHTS))]
    whole = features[:, 0, :]
    current = []
    result = None
    for layer in range(layers):
        info = jnp.stack([counts[layer], there >> 2, there & 3])
        after, gate, earlier = [], [], []
        for c, height in enumerate(HEIGHTS):
            if layer == 0:
                current.append(take(whole, firsts[c], height, after))
            parts = gather(current[c], gate)
            after = [] if GATHER == 'sc' else parts[3 : N_ROW // 2 : 2]
            sums = product(
                layer, (absolute if GATHER == 'sc' else place)[layer], col[layer], info, parts, block_values, height, earlier
            )
            gate = [sums[0]] if GATE else []
            away = [sums[N_Y]] + [
                lax.ppermute(sums[N_Y + d], "col", to_y(d)) for d in range(1, N_Y)
            ]
            sent = middle(away)
            earlier = [sent] if ORDER else []
            other = lax.ppermute(sent, "col", TO_Z_HI)
            pieces = [sums[0]] + [lax.ppermute(sums[d], "col", to_y(d)) for d in range(1, N_Y)]
            if layer < layers - 1:
                current[c] = combine(pieces, other, bias[layer])
            else:
                result = finish(pieces, other, bias[layer], firsts[c], batch, result)
    return result[:, None, :]


def solution(mesh):
    in_specs = (
        P(None, "col", "row"),
        P(None, "row", "col", None, None, None),
        P(None, "row", "col", None),
        P(None, "row", "col", None),
        P(None, "row", "col"),
        P(None, "col", "row"),
    )
    out_specs = P(None, "col", "row")
    return jax.shard_map(
        on_device, mesh=mesh, in_specs=in_specs, out_specs=out_specs, check_vma=False
    )
```

```python
import functools

import jax
import jax.numpy as jnp
from jax import lax
from jax.experimental import pallas as pl
from jax.experimental.pallas import tpu as pltpu
from jax.sharding import PartitionSpec as P

BLK = 128
CB = 32
N_ROW = 16
N_COL = 8
N_Y = 4
SUB = CB // N_COL
HALF = CB // 2
GROUP = 16
ROW_AT, COLUMN_AT = 9, 15
HEIGHTS = (256, 256)
STEPS = 16.0
TOP = 32000.0
VMEM = pl.BlockSpec(memory_space=pltpu.VMEM)
SMEM = pl.BlockSpec(memory_space=pltpu.SMEM)
ANY = pl.BlockSpec(memory_space=pl.ANY)
HBM = pl.BlockSpec(memory_space=pltpu.HBM)

def to_col(e, d):
    return [(c, ((c & 4) ^ (4 * e)) + ((c + d) & 3)) for c in range(N_COL)]


def plan(block_rows, block_cols, counts, z_hi, y):
    slots = block_cols.shape[1]
    index = jnp.arange(slots, dtype=jnp.int32)
    live = index[None, :] < counts[:, None]
    apart_z = (block_cols >> 4) ^ z_hi
    apart_y = ((block_cols >> 2) - y) & (N_Y - 1)
    column = apart_y * SUB + (block_cols & (SUB - 1))
    code = index[None, :] | (block_rows << ROW_AT) | (column << COLUMN_AT)
    unused = HALF << COLUMN_AT
    halves = jnp.arange(2, dtype=jnp.int32)[None, :, None]
    member = live[:, None, :] & (apart_z[:, None, :] == halves)
    lower = index[None, :] < index[:, None]
    rank = jnp.sum(member[:, :, None, :] & lower[None, None], axis=3, dtype=jnp.int32)
    at = (member & (rank < slots))[:, :, None, :] & (
        rank[:, :, None, :] == index[None, None, :, None]
    )
    codes = unused + jnp.sum(jnp.where(at, code[:, None, None, :] - unused, 0), axis=3)
    return codes, jnp.sum(member, axis=2, dtype=jnp.int32)


def product_kernel(layer, codes, count, gathered, values, *refs):
    *outs, panel, held, acc, part_sem, sems = refs[-N_Y - 5 :]
    height = panel.shape[1]
    groups = (count[0] + GROUP - 1) // GROUP
    ahead = 4

    def fetch(group):
        @pl.when(group < groups)
        def _():
            for j in range(GROUP):
                spot = group * GROUP + j
                slot = codes[spot] & ((1 << ROW_AT) - 1)
                pltpu.make_async_copy(
                    values.at[layer, 0, 0, slot], held.at[spot], sems.at[group]
                ).start()

    whole = pltpu.make_async_copy(gathered, panel, part_sem)
    whole.start()
    for group in range(ahead):
        fetch(group)
    acc[...] = jnp.zeros_like(acc)
    whole.wait()

    def one_group(group, _):
        fetch(group + ahead)
        spots = pl.ds(group * GROUP, GROUP)
        pltpu.make_async_copy(
            values.at[layer, 0, 0, pl.ds(0, GROUP)], held.at[spots], sems.at[group]
        ).wait()
        for j in range(GROUP):
            spot = group * GROUP + j
            code = codes[spot]
            row = (code >> ROW_AT) & ((1 << (COLUMN_AT - ROW_AT)) - 1)
            lanes = pl.ds(pl.multiple_of((row & (SUB - 1)) * BLK, BLK), BLK)
            left = panel[row >> 2, :, lanes]
            acc[code >> COLUMN_AT] += jnp.dot(
                left, held[spot], preferred_element_type=jnp.float32
            )
        return 0

    lax.fori_loop(0, groups, one_group, 0)
    for d in range(N_Y):
        encode(lambda t, d=d: acc[d * SUB + t], outs[d], height)


def encode(sums_of, out, height):
    codes = []
    for t in range(SUB):
        sums = sums_of(t)
        most = jnp.max(jnp.abs(sums), axis=0, keepdims=True)
        code = jnp.ceil(jnp.log2(jnp.maximum(most, 1e-30)) * STEPS)
        codes.append(code)
        inverse = TOP * jnp.exp2(code * (-1.0 / STEPS))
        whole = jnp.round(sums * inverse).astype(jnp.int32)
        out[pl.ds(t * height, height), :] = whole.astype(jnp.int16)
    codes = jnp.concatenate(codes + [jnp.zeros((16 - SUB, BLK), jnp.float32)], axis=0)
    out[pl.ds(SUB * height, 16), :] = codes.astype(jnp.int32).astype(jnp.int16)


def product(layer, codes, count, gathered, values, after=()):
    slots, height = values.shape[3], gathered.shape[1]
    piece = jax.ShapeDtypeStruct((SUB * height + 16, BLK), jnp.int16)
    return pl.pallas_call(
        functools.partial(product_kernel, layer),
        out_shape=(piece,) * N_Y,
        in_specs=[SMEM] * 2 + [HBM] * 2 + [ANY] * len(after),
        out_specs=(VMEM,) * N_Y,
        scratch_shapes=[
            pltpu.VMEM((N_ROW, height, SUB * BLK), jnp.bfloat16),
            pltpu.VMEM((slots, BLK, BLK), jnp.bfloat16),
            pltpu.VMEM((HALF + 1, height, BLK), jnp.float32),
            pltpu.SemaphoreType.DMA,
            pltpu.SemaphoreType.DMA((slots // GROUP,)),
        ],
        compiler_params=pltpu.CompilerParams(vmem_limit_bytes=58 * 1024 * 1024),
        cost_estimate=pl.CostEstimate(
            flops=8 * height * BLK * BLK * slots,
            bytes_accessed=slots * BLK * BLK * 2,
            transcendentals=0,
        ),
        name="product",
    )(codes, count, gathered, values, *after)


def rows_at_once(height):
    return next(r for r in (64, 48, 32, 16) if height % r == 0)


def scales_of(piece, height):
    codes = piece[pl.ds(SUB * height, 16), :].astype(jnp.int32).astype(jnp.float32)
    return jnp.exp2(codes * (1.0 / STEPS)) * (1.0 / TOP)


def add_pieces(pieces, scales, t, spot):
    total = None
    for piece, scale in zip(pieces, scales):
        term = piece[spot, :].astype(jnp.int32).astype(jnp.float32) * scale[t : t + 1, :]
        total = term if total is None else total + term
    return total


def middle_kernel(a, b, c, d, out, totals):
    height = totals.shape[0]
    rows = rows_at_once(height)
    pieces = (a, b, c, d)
    scales = [scales_of(piece, height) for piece in pieces]
    codes = []
    for t in range(SUB):

        def add(i, most, t=t):
            first = pl.multiple_of(i * rows, rows)
            total = add_pieces(pieces, scales, t, pl.ds(t * height + first, rows))
            totals[pl.ds(first, rows), :] = total
            return jnp.maximum(most, jnp.max(jnp.abs(total).reshape(rows // 8, 8, BLK), axis=0))

        most = lax.fori_loop(0, height // rows, add, jnp.zeros((8, BLK), jnp.float32))
        most = jnp.max(most, axis=0, keepdims=True)
        code = jnp.ceil(jnp.log2(jnp.maximum(most, 1e-30)) * STEPS)
        codes.append(code)
        inverse = TOP * jnp.exp2(code * (-1.0 / STEPS))

        def store(i, _, t=t, inverse=inverse):
            first = pl.multiple_of(i * rows, rows)
            whole = jnp.round(totals[pl.ds(first, rows), :] * inverse).astype(jnp.int32)
            out[pl.ds(t * height + first, rows), :] = whole.astype(jnp.int16)
            return 0

        lax.fori_loop(0, height // rows, store, 0)
    codes = jnp.concatenate(codes + [jnp.zeros((16 - SUB, BLK), jnp.float32)], axis=0)
    out[pl.ds(SUB * height, 16), :] = codes.astype(jnp.int32).astype(jnp.int16)


def middle(pieces):
    height = (pieces[0].shape[0] - 16) // SUB
    return pl.pallas_call(
        middle_kernel,
        out_shape=jax.ShapeDtypeStruct(pieces[0].shape, jnp.int16),
        in_specs=[VMEM] * 4,
        out_specs=VMEM,
        scratch_shapes=[pltpu.VMEM((height, BLK), jnp.float32)],
        cost_estimate=pl.CostEstimate(
            flops=16 * pieces[0].size, bytes_accessed=8 * pieces[0].size, transcendentals=0
        ),
        name="middle",
    )(*pieces)


def add_and_clip(pieces, bias, out, height):
    rows = rows_at_once(height)
    scales = [scales_of(piece, height) for piece in pieces]
    for t in range(SUB):
        lanes = slice(t * BLK, (t + 1) * BLK)

        def part(i, _, t=t, lanes=lanes):
            first = pl.multiple_of(i * rows, rows)
            total = add_pieces(pieces, scales, t, pl.ds(t * height + first, rows)) + bias[:, lanes]
            kept = jnp.minimum(jnp.maximum(total, 0.0), 32.0)
            out[pl.ds(first, rows), lanes] = kept.astype(jnp.bfloat16)
            return 0

        lax.fori_loop(0, height // rows, part, 0)


def combine_kernel(n_pieces, first, *refs):
    pieces, bias, (out, kept, sem) = refs[:n_pieces], refs[n_pieces], refs[-3:]
    height = kept.shape[0]
    add_and_clip(pieces, bias, kept, height)
    copy = pltpu.make_async_copy(kept, out.at[pl.ds(first, height)], sem)
    copy.start()
    copy.wait()


def combine(pieces, bias, first=0, batch=None, earlier=None):
    height = (pieces[0].shape[0] - 16) // SUB
    more = [] if earlier is None else [earlier]
    n_pieces = len(pieces)
    return pl.pallas_call(
        functools.partial(combine_kernel, n_pieces, first),
        out_shape=jax.ShapeDtypeStruct((batch or height, SUB * BLK), jnp.bfloat16),
        in_specs=[VMEM] * (n_pieces + 1) + [ANY] * len(more),
        out_specs=HBM,
        scratch_shapes=[
            pltpu.VMEM((height, SUB * BLK), jnp.bfloat16),
            pltpu.SemaphoreType.DMA,
        ],
        input_output_aliases={n_pieces + 1: 0} if more else {},
        cost_estimate=pl.CostEstimate(
            flops=16 * pieces[0].size, bytes_accessed=10 * pieces[0].size, transcendentals=0
        ),
        name="combine",
    )(*pieces, bias, *more)


def exchange(layer, codes, counts, gathered, values, after):
    far = product(layer, codes[1], counts[1:], gathered, values, after)
    away = [far[0]] + [lax.ppermute(far[d], "col", to_col(0, d)) for d in range(1, N_Y)]
    near = product(layer, codes[0], counts[:1], gathered, values)
    sent = middle(away)
    pieces = [near[0], lax.ppermute(sent, "col", to_col(1, 0))]
    pieces += [lax.ppermute(near[d], "col", to_col(0, d)) for d in range(1, N_Y)]
    return pieces, [sent, near[0]]


def on_device(features, block_values, block_rows, block_cols, block_counts, bias):
    layers = block_values.shape[0]
    batch = features.shape[0]
    there = lax.axis_index("col")
    codes, counts = plan(
        block_rows[:, 0, 0], block_cols[:, 0, 0], block_counts[:, 0, 0], there >> 2, there & 3
    )
    firsts = [sum(HEIGHTS[:c]) for c in range(len(HEIGHTS))]
    current = [features[f : f + h, 0, :] for f, h in zip(firsts, HEIGHTS)]
    result = None
    for layer in range(layers):
        after = []
        for c in range(len(HEIGHTS)):
            gathered = lax.all_gather(current[c], "row", axis=0, tiled=False)
            pieces, sent = exchange(
                layer, codes[layer], counts[layer], gathered, block_values, after
            )
            after = sent
            if layer < layers - 1:
                current[c] = combine(pieces, bias[layer])
            else:
                result = combine(pieces, bias[layer], firsts[c], batch, result)
                after = [result]
    return result[:, None, :]


def solution(mesh):
    in_specs = (
        P(None, "col", "row"),
        P(None, "row", "col", None, None, None),
        P(None, "row", "col", None),
        P(None, "row", "col", None),
        P(None, "row", "col"),
        P(None, "col", "row"),
    )
    out_specs = P(None, "col", "row")
    return jax.shard_map(
        on_device, mesh=mesh, in_specs=in_specs, out_specs=out_specs, check_vma=False
    )
```

```python
import functools

import jax
import jax.numpy as jnp
from jax import lax
from jax.experimental import pallas as pl
from jax.experimental.pallas import tpu as pltpu
from jax.sharding import PartitionSpec as P

BLK = 128
CB = 32
N_ROW = 16
N_COL = 8
N_Y = 4
SUB = CB // N_COL
HALF = CB // 2
GROUP = 32
ROW_AT, COLUMN_AT = 9, 15
HEIGHTS = (256, 256)
STEPS = 16.0
TOP = 32000.0
VMEM = pl.BlockSpec(memory_space=pltpu.VMEM)
SMEM = pl.BlockSpec(memory_space=pltpu.SMEM)
ANY = pl.BlockSpec(memory_space=pl.ANY)
HBM = pl.BlockSpec(memory_space=pltpu.HBM)

def to_col(e, d):
    return [(c, ((c & 4) ^ (4 * e)) + ((c + d) & 3)) for c in range(N_COL)]


def plan(block_rows, block_cols, counts, z_hi, y):
    slots = block_cols.shape[1]
    index = jnp.arange(slots, dtype=jnp.int32)
    live = index[None, :] < counts[:, None]
    apart_z = (block_cols >> 4) ^ z_hi
    apart_y = ((block_cols >> 2) - y) & (N_Y - 1)
    column = apart_y * SUB + (block_cols & (SUB - 1))
    code = index[None, :] | (block_rows << ROW_AT) | (column << COLUMN_AT)
    unused = HALF << COLUMN_AT
    halves = jnp.arange(2, dtype=jnp.int32)[None, :, None]
    member = live[:, None, :] & (apart_z[:, None, :] == halves)
    lower = index[None, :] < index[:, None]
    rank = jnp.sum(member[:, :, None, :] & lower[None, None], axis=3, dtype=jnp.int32)
    at = (member & (rank < slots))[:, :, None, :] & (
        rank[:, :, None, :] == index[None, None, :, None]
    )
    codes = unused + jnp.sum(jnp.where(at, code[:, None, None, :] - unused, 0), axis=3)
    return codes, jnp.sum(member, axis=2, dtype=jnp.int32)


def product_kernel(layer, codes, count, gathered, values, *refs):
    *outs, panel, held, acc, part_sem, sems = refs[-N_Y - 5 :]
    height = panel.shape[1]
    groups = (count[0] + GROUP - 1) // GROUP
    ahead = 2

    def fetch(group):
        @pl.when(group < groups)
        def _():
            for j in range(GROUP):
                spot = group * GROUP + j
                slot = codes[spot] & ((1 << ROW_AT) - 1)
                pltpu.make_async_copy(
                    values.at[layer, 0, 0, slot], held.at[spot], sems.at[group]
                ).start()

    whole = pltpu.make_async_copy(gathered, panel, part_sem)
    whole.start()
    for group in range(ahead):
        fetch(group)
    acc[...] = jnp.zeros_like(acc)
    whole.wait()

    def one_group(group, _):
        fetch(group + ahead)
        spots = pl.ds(group * GROUP, GROUP)
        pltpu.make_async_copy(
            values.at[layer, 0, 0, pl.ds(0, GROUP)], held.at[spots], sems.at[group]
        ).wait()
        for j in range(GROUP):
            spot = group * GROUP + j
            code = codes[spot]
            row = (code >> ROW_AT) & ((1 << (COLUMN_AT - ROW_AT)) - 1)
            lanes = pl.ds(pl.multiple_of((row & (SUB - 1)) * BLK, BLK), BLK)
            left = panel[row >> 2, :, lanes]
            acc[code >> COLUMN_AT] += jnp.dot(
                left, held[spot], preferred_element_type=jnp.float32
            )
        return 0

    lax.fori_loop(0, groups, one_group, 0)
    for d in range(N_Y):
        encode(lambda t, d=d: acc[d * SUB + t], outs[d], height)


def encode(sums_of, out, height):
    codes = []
    for t in range(SUB):
        sums = sums_of(t)
        most = jnp.max(jnp.abs(sums), axis=0, keepdims=True)
        code = jnp.ceil(jnp.log2(jnp.maximum(most, 1e-30)) * STEPS)
        codes.append(code)
        inverse = TOP * jnp.exp2(code * (-1.0 / STEPS))
        whole = jnp.round(sums * inverse).astype(jnp.int32)
        out[pl.ds(t * height, height), :] = whole.astype(jnp.int16)
    codes = jnp.concatenate(codes + [jnp.zeros((16 - SUB, BLK), jnp.float32)], axis=0)
    out[pl.ds(SUB * height, 16), :] = codes.astype(jnp.int32).astype(jnp.int16)


def product(layer, codes, count, gathered, values, after=()):
    slots, height = values.shape[3], gathered.shape[1]
    piece = jax.ShapeDtypeStruct((SUB * height + 16, BLK), jnp.int16)
    return pl.pallas_call(
        functools.partial(product_kernel, layer),
        out_shape=(piece,) * N_Y,
        in_specs=[SMEM] * 2 + [HBM] * 2 + [ANY] * len(after),
        out_specs=(VMEM,) * N_Y,
        scratch_shapes=[
            pltpu.VMEM((N_ROW, height, SUB * BLK), jnp.bfloat16),
            pltpu.VMEM((slots, BLK, BLK), jnp.bfloat16),
            pltpu.VMEM((HALF + 1, height, BLK), jnp.float32),
            pltpu.SemaphoreType.DMA,
            pltpu.SemaphoreType.DMA((slots // GROUP,)),
        ],
        compiler_params=pltpu.CompilerParams(vmem_limit_bytes=58 * 1024 * 1024),
        cost_estimate=pl.CostEstimate(
            flops=8 * height * BLK * BLK * slots,
            bytes_accessed=slots * BLK * BLK * 2,
            transcendentals=0,
        ),
        name="product",
    )(codes, count, gathered, values, *after)


def rows_at_once(height):
    return next(r for r in (64, 48, 32, 16) if height % r == 0)


def scales_of(piece, height):
    codes = piece[pl.ds(SUB * height, 16), :].astype(jnp.int32).astype(jnp.float32)
    return jnp.exp2(codes * (1.0 / STEPS)) * (1.0 / TOP)


def add_pieces(pieces, scales, t, spot):
    total = None
    for piece, scale in zip(pieces, scales):
        term = piece[spot, :].astype(jnp.int32).astype(jnp.float32) * scale[t : t + 1, :]
        total = term if total is None else total + term
    return total


def middle_kernel(a, b, c, d, out, totals):
    height = totals.shape[0]
    rows = rows_at_once(height)
    pieces = (a, b, c, d)
    scales = [scales_of(piece, height) for piece in pieces]
    codes = []
    for t in range(SUB):

        def add(i, most, t=t):
            first = pl.multiple_of(i * rows, rows)
            total = add_pieces(pieces, scales, t, pl.ds(t * height + first, rows))
            totals[pl.ds(first, rows), :] = total
            return jnp.maximum(most, jnp.max(jnp.abs(total).reshape(rows // 8, 8, BLK), axis=0))

        most = lax.fori_loop(0, height // rows, add, jnp.zeros((8, BLK), jnp.float32))
        most = jnp.max(most, axis=0, keepdims=True)
        code = jnp.ceil(jnp.log2(jnp.maximum(most, 1e-30)) * STEPS)
        codes.append(code)
        inverse = TOP * jnp.exp2(code * (-1.0 / STEPS))

        def store(i, _, t=t, inverse=inverse):
            first = pl.multiple_of(i * rows, rows)
            whole = jnp.round(totals[pl.ds(first, rows), :] * inverse).astype(jnp.int32)
            out[pl.ds(t * height + first, rows), :] = whole.astype(jnp.int16)
            return 0

        lax.fori_loop(0, height // rows, store, 0)
    codes = jnp.concatenate(codes + [jnp.zeros((16 - SUB, BLK), jnp.float32)], axis=0)
    out[pl.ds(SUB * height, 16), :] = codes.astype(jnp.int32).astype(jnp.int16)


def middle(pieces):
    height = (pieces[0].shape[0] - 16) // SUB
    return pl.pallas_call(
        middle_kernel,
        out_shape=jax.ShapeDtypeStruct(pieces[0].shape, jnp.int16),
        in_specs=[VMEM] * 4,
        out_specs=VMEM,
        scratch_shapes=[pltpu.VMEM((height, BLK), jnp.float32)],
        cost_estimate=pl.CostEstimate(
            flops=16 * pieces[0].size, bytes_accessed=8 * pieces[0].size, transcendentals=0
        ),
        name="middle",
    )(*pieces)


def add_and_clip(pieces, bias, out, height):
    rows = rows_at_once(height)
    scales = [scales_of(piece, height) for piece in pieces]
    for t in range(SUB):
        lanes = slice(t * BLK, (t + 1) * BLK)

        def part(i, _, t=t, lanes=lanes):
            first = pl.multiple_of(i * rows, rows)
            total = add_pieces(pieces, scales, t, pl.ds(t * height + first, rows)) + bias[:, lanes]
            kept = jnp.minimum(jnp.maximum(total, 0.0), 32.0)
            out[pl.ds(first, rows), lanes] = kept.astype(jnp.bfloat16)
            return 0

        lax.fori_loop(0, height // rows, part, 0)


def combine_kernel(n_pieces, first, *refs):
    pieces, bias, (out, kept, sem) = refs[:n_pieces], refs[n_pieces], refs[-3:]
    height = kept.shape[0]
    add_and_clip(pieces, bias, kept, height)
    copy = pltpu.make_async_copy(kept, out.at[pl.ds(first, height)], sem)
    copy.start()
    copy.wait()


def combine(pieces, bias, first=0, batch=None, earlier=None):
    height = (pieces[0].shape[0] - 16) // SUB
    more = [] if earlier is None else [earlier]
    n_pieces = len(pieces)
    return pl.pallas_call(
        functools.partial(combine_kernel, n_pieces, first),
        out_shape=jax.ShapeDtypeStruct((batch or height, SUB * BLK), jnp.bfloat16),
        in_specs=[VMEM] * (n_pieces + 1) + [ANY] * len(more),
        out_specs=HBM,
        scratch_shapes=[
            pltpu.VMEM((height, SUB * BLK), jnp.bfloat16),
            pltpu.SemaphoreType.DMA,
        ],
        input_output_aliases={n_pieces + 1: 0} if more else {},
        cost_estimate=pl.CostEstimate(
            flops=16 * pieces[0].size, bytes_accessed=10 * pieces[0].size, transcendentals=0
        ),
        name="combine",
    )(*pieces, bias, *more)


def exchange(layer, codes, counts, gathered, values, after):
    far = product(layer, codes[1], counts[1:], gathered, values, after)
    away = [far[0]] + [lax.ppermute(far[d], "col", to_col(0, d)) for d in range(1, N_Y)]
    near = product(layer, codes[0], counts[:1], gathered, values)
    sent = middle(away)
    pieces = [near[0], lax.ppermute(sent, "col", to_col(1, 0))]
    pieces += [lax.ppermute(near[d], "col", to_col(0, d)) for d in range(1, N_Y)]
    return pieces, [sent, near[0]]


def on_device(features, block_values, block_rows, block_cols, block_counts, bias):
    layers = block_values.shape[0]
    batch = features.shape[0]
    there = lax.axis_index("col")
    codes, counts = plan(
        block_rows[:, 0, 0], block_cols[:, 0, 0], block_counts[:, 0, 0], there >> 2, there & 3
    )
    firsts = [sum(HEIGHTS[:c]) for c in range(len(HEIGHTS))]
    current = [features[f : f + h, 0, :] for f, h in zip(firsts, HEIGHTS)]
    result = None
    for layer in range(layers):
        after = []
        for c in range(len(HEIGHTS)):
            gathered = lax.all_gather(current[c], "row", axis=0, tiled=False)
            pieces, sent = exchange(
                layer, codes[layer], counts[layer], gathered, block_values, after
            )
            after = sent
            if layer < layers - 1:
                current[c] = combine(pieces, bias[layer])
            else:
                result = combine(pieces, bias[layer], firsts[c], batch, result)
                after = after + pieces[2:]
    return result[:, None, :]


def solution(mesh):
    in_specs = (
        P(None, "col", "row"),
        P(None, "row", "col", None, None, None),
        P(None, "row", "col", None),
        P(None, "row", "col", None),
        P(None, "row", "col"),
        P(None, "col", "row"),
    )
    out_specs = P(None, "col", "row")
    return jax.shard_map(
        on_device, mesh=mesh, in_specs=in_specs, out_specs=out_specs, check_vma=False
    )
```

```python
import functools

import jax
import jax.numpy as jnp
from jax import lax
from jax.experimental import pallas as pl
from jax.experimental.pallas import tpu as pltpu
from jax.sharding import PartitionSpec as P

BLK = 128
CB = 32
N_ROW = 16
N_COL = 8
N_Y = 4
SUB = CB // N_COL
HALF = CB // 2
GROUP = 32
ROW_AT, COLUMN_AT = 9, 15
HEIGHTS = (256, 256)
STEPS = 16.0
TOP = 32000.0
VMEM = pl.BlockSpec(memory_space=pltpu.VMEM)
SMEM = pl.BlockSpec(memory_space=pltpu.SMEM)
ANY = pl.BlockSpec(memory_space=pl.ANY)
HBM = pl.BlockSpec(memory_space=pltpu.HBM)

def to_col(e, d):
    return [(c, ((c & 4) ^ (4 * e)) + ((c + d) & 3)) for c in range(N_COL)]


def plan(block_rows, block_cols, counts, z_hi, y):
    slots = block_cols.shape[1]
    index = jnp.arange(slots, dtype=jnp.int32)
    live = index[None, :] < counts[:, None]
    apart_z = (block_cols >> 4) ^ z_hi
    apart_y = ((block_cols >> 2) - y) & (N_Y - 1)
    column = apart_y * SUB + (block_cols & (SUB - 1))
    code = index[None, :] | (block_rows << ROW_AT) | (column << COLUMN_AT)
    unused = HALF << COLUMN_AT
    halves = jnp.arange(2, dtype=jnp.int32)[None, :, None]
    member = live[:, None, :] & (apart_z[:, None, :] == halves)
    lower = index[None, :] < index[:, None]
    rank = jnp.sum(member[:, :, None, :] & lower[None, None], axis=3, dtype=jnp.int32)
    at = (member & (rank < slots))[:, :, None, :] & (
        rank[:, :, None, :] == index[None, None, :, None]
    )
    codes = unused + jnp.sum(jnp.where(at, code[:, None, None, :] - unused, 0), axis=3)
    return codes, jnp.sum(member, axis=2, dtype=jnp.int32)


def product_kernel(layer, codes, count, gathered, values, *refs):
    *outs, panel, held, acc, part_sem, sems = refs[-N_Y - 5 :]
    height = panel.shape[1]
    groups = (count[0] + GROUP - 1) // GROUP
    ahead = 2

    def fetch(group):
        @pl.when(group < groups)
        def _():
            for j in range(GROUP):
                spot = group * GROUP + j
                slot = codes[spot] & ((1 << ROW_AT) - 1)
                pltpu.make_async_copy(
                    values.at[layer, 0, 0, slot], held.at[spot], sems.at[group]
                ).start()

    whole = pltpu.make_async_copy(gathered, panel, part_sem)
    whole.start()
    for group in range(ahead):
        fetch(group)
    acc[...] = jnp.zeros_like(acc)
    whole.wait()

    def one_group(group, _):
        fetch(group + ahead)
        spots = pl.ds(group * GROUP, GROUP)
        pltpu.make_async_copy(
            values.at[layer, 0, 0, pl.ds(0, GROUP)], held.at[spots], sems.at[group]
        ).wait()
        for j in range(GROUP):
            spot = group * GROUP + j
            code = codes[spot]
            row = (code >> ROW_AT) & ((1 << (COLUMN_AT - ROW_AT)) - 1)
            lanes = pl.ds(pl.multiple_of((row & (SUB - 1)) * BLK, BLK), BLK)
            left = panel[row >> 2, :, lanes]
            acc[code >> COLUMN_AT] += jnp.dot(
                left, held[spot], preferred_element_type=jnp.float32
            )
        return 0

    lax.fori_loop(0, groups, one_group, 0)
    for d in range(N_Y):
        encode(lambda t, d=d: acc[d * SUB + t], outs[d], height)


def encode(sums_of, out, height):
    codes = []
    for t in range(SUB):
        sums = sums_of(t)
        most = jnp.max(jnp.abs(sums), axis=0, keepdims=True)
        code = jnp.ceil(jnp.log2(jnp.maximum(most, 1e-30)) * STEPS)
        codes.append(code)
        inverse = TOP * jnp.exp2(code * (-1.0 / STEPS))
        whole = jnp.round(sums * inverse).astype(jnp.int32)
        out[pl.ds(t * height, height), :] = whole.astype(jnp.int16)
    codes = jnp.concatenate(codes + [jnp.zeros((16 - SUB, BLK), jnp.float32)], axis=0)
    out[pl.ds(SUB * height, 16), :] = codes.astype(jnp.int32).astype(jnp.int16)


def product(layer, codes, count, gathered, values, after=()):
    slots, height = values.shape[3], gathered.shape[1]
    piece = jax.ShapeDtypeStruct((SUB * height + 16, BLK), jnp.int16)
    return pl.pallas_call(
        functools.partial(product_kernel, layer),
        out_shape=(piece,) * N_Y,
        in_specs=[SMEM] * 2 + [HBM] * 2 + [ANY] * len(after),
        out_specs=(VMEM,) * N_Y,
        scratch_shapes=[
            pltpu.VMEM((N_ROW, height, SUB * BLK), jnp.bfloat16),
            pltpu.VMEM((slots, BLK, BLK), jnp.bfloat16),
            pltpu.VMEM((HALF + 1, height, BLK), jnp.float32),
            pltpu.SemaphoreType.DMA,
            pltpu.SemaphoreType.DMA((slots // GROUP,)),
        ],
        compiler_params=pltpu.CompilerParams(vmem_limit_bytes=58 * 1024 * 1024),
        cost_estimate=pl.CostEstimate(
            flops=8 * height * BLK * BLK * slots,
            bytes_accessed=slots * BLK * BLK * 2,
            transcendentals=0,
        ),
        name="product",
    )(codes, count, gathered, values, *after)


def rows_at_once(height):
    return next(r for r in (256, 64, 48, 32, 16) if height % r == 0)


def scales_of(piece, height):
    codes = piece[pl.ds(SUB * height, 16), :].astype(jnp.int32).astype(jnp.float32)
    return jnp.exp2(codes * (1.0 / STEPS)) * (1.0 / TOP)


def add_pieces(pieces, scales, t, spot):
    total = None
    for piece, scale in zip(pieces, scales):
        term = piece[spot, :].astype(jnp.int32).astype(jnp.float32) * scale[t : t + 1, :]
        total = term if total is None else total + term
    return total


def middle_kernel(a, b, c, d, out, totals):
    height = totals.shape[0]
    rows = rows_at_once(height)
    pieces = (a, b, c, d)
    scales = [scales_of(piece, height) for piece in pieces]
    codes = []
    for t in range(SUB):

        def add(i, most, t=t):
            first = pl.multiple_of(i * rows, rows)
            total = add_pieces(pieces, scales, t, pl.ds(t * height + first, rows))
            totals[pl.ds(first, rows), :] = total
            return jnp.maximum(most, jnp.max(jnp.abs(total).reshape(rows // 8, 8, BLK), axis=0))

        most = lax.fori_loop(0, height // rows, add, jnp.zeros((8, BLK), jnp.float32))
        most = jnp.max(most, axis=0, keepdims=True)
        code = jnp.ceil(jnp.log2(jnp.maximum(most, 1e-30)) * STEPS)
        codes.append(code)
        inverse = TOP * jnp.exp2(code * (-1.0 / STEPS))

        def store(i, _, t=t, inverse=inverse):
            first = pl.multiple_of(i * rows, rows)
            whole = jnp.round(totals[pl.ds(first, rows), :] * inverse).astype(jnp.int32)
            out[pl.ds(t * height + first, rows), :] = whole.astype(jnp.int16)
            return 0

        lax.fori_loop(0, height // rows, store, 0)
    codes = jnp.concatenate(codes + [jnp.zeros((16 - SUB, BLK), jnp.float32)], axis=0)
    out[pl.ds(SUB * height, 16), :] = codes.astype(jnp.int32).astype(jnp.int16)


def middle(pieces):
    height = (pieces[0].shape[0] - 16) // SUB
    return pl.pallas_call(
        middle_kernel,
        out_shape=jax.ShapeDtypeStruct(pieces[0].shape, jnp.int16),
        in_specs=[VMEM] * 4,
        out_specs=VMEM,
        scratch_shapes=[pltpu.VMEM((height, BLK), jnp.float32)],
        cost_estimate=pl.CostEstimate(
            flops=16 * pieces[0].size, bytes_accessed=8 * pieces[0].size, transcendentals=0
        ),
        name="middle",
    )(*pieces)


def add_and_clip(pieces, bias, out, height):
    rows = rows_at_once(height)
    scales = [scales_of(piece, height) for piece in pieces]
    for t in range(SUB):
        lanes = slice(t * BLK, (t + 1) * BLK)

        def part(i, _, t=t, lanes=lanes):
            first = pl.multiple_of(i * rows, rows)
            total = add_pieces(pieces, scales, t, pl.ds(t * height + first, rows)) + bias[:, lanes]
            kept = jnp.minimum(jnp.maximum(total, 0.0), 32.0)
            out[pl.ds(first, rows), lanes] = kept.astype(jnp.bfloat16)
            return 0

        lax.fori_loop(0, height // rows, part, 0)


def combine_kernel(n_pieces, first, *refs):
    pieces, bias, (out, kept, sem) = refs[:n_pieces], refs[n_pieces], refs[-3:]
    height = kept.shape[0]
    add_and_clip(pieces, bias, kept, height)
    copy = pltpu.make_async_copy(kept, out.at[pl.ds(first, height)], sem)
    copy.start()
    copy.wait()


def combine(pieces, bias, first=0, batch=None, earlier=None):
    height = (pieces[0].shape[0] - 16) // SUB
    more = [] if earlier is None else [earlier]
    n_pieces = len(pieces)
    return pl.pallas_call(
        functools.partial(combine_kernel, n_pieces, first),
        out_shape=jax.ShapeDtypeStruct((batch or height, SUB * BLK), jnp.bfloat16),
        in_specs=[VMEM] * (n_pieces + 1) + [ANY] * len(more),
        out_specs=HBM,
        scratch_shapes=[
            pltpu.VMEM((height, SUB * BLK), jnp.bfloat16),
            pltpu.SemaphoreType.DMA,
        ],
        input_output_aliases={n_pieces + 1: 0} if more else {},
        cost_estimate=pl.CostEstimate(
            flops=16 * pieces[0].size, bytes_accessed=10 * pieces[0].size, transcendentals=0
        ),
        name="combine",
    )(*pieces, bias, *more)


def exchange(layer, codes, counts, gathered, values, after):
    far = product(layer, codes[1], counts[1:], gathered, values, after)
    away = [far[0]] + [lax.ppermute(far[d], "col", to_col(0, d)) for d in range(1, N_Y)]
    near = product(layer, codes[0], counts[:1], gathered, values)
    sent = middle(away)
    pieces = [near[0], lax.ppermute(sent, "col", to_col(1, 0))]
    pieces += [lax.ppermute(near[d], "col", to_col(0, d)) for d in range(1, N_Y)]
    return pieces, [sent, near[0]]


def on_device(features, block_values, block_rows, block_cols, block_counts, bias):
    layers = block_values.shape[0]
    batch = features.shape[0]
    there = lax.axis_index("col")
    codes, counts = plan(
        block_rows[:, 0, 0], block_cols[:, 0, 0], block_counts[:, 0, 0], there >> 2, there & 3
    )
    firsts = [sum(HEIGHTS[:c]) for c in range(len(HEIGHTS))]
    current = [features[f : f + h, 0, :] for f, h in zip(firsts, HEIGHTS)]
    result = None
    for layer in range(layers):
        after = []
        for c in range(len(HEIGHTS)):
            gathered = lax.all_gather(current[c], "row", axis=0, tiled=False)
            pieces, sent = exchange(
                layer, codes[layer], counts[layer], gathered, block_values, after
            )
            after = sent
            if layer < layers - 1:
                current[c] = combine(pieces, bias[layer])
            else:
                result = combine(pieces, bias[layer], firsts[c], batch, result)
                after = after + pieces[2:]
    return result[:, None, :]


def solution(mesh):
    in_specs = (
        P(None, "col", "row"),
        P(None, "row", "col", None, None, None),
        P(None, "row", "col", None),
        P(None, "row", "col", None),
        P(None, "row", "col"),
        P(None, "col", "row"),
    )
    out_specs = P(None, "col", "row")
    return jax.shard_map(
        on_device, mesh=mesh, in_specs=in_specs, out_specs=out_specs, check_vma=False
    )
```
